32 devices in a mesh: groups: 2 (over y), date: 8 (over z, x), pix: 2 (over core).
Axes of the slice: x: 2, y: 2, z: 4, core: 2. Of those that a mesh axis runs over, the one named last changes fastest.
Arguments:
- slc_tiles: bfloat16 [32, 2, 64, 1024], P(('groups', 'date'), None, None, 'pix'), parts along dimension 0, may hold values from -8 to 8
- pair_list: int32 [128, 2], P(('groups', 'date')), parts along dimension 0, may hold values from 0 to 15, as said below
- band_cuts: int32 [128, 2], P(('groups', 'date')), parts along dimension 0, may hold values from 0 to 127
- look_sizes: int32 [128, 2], P(('groups', 'date')), parts along dimension 0, may hold values from 1 to 16, as said below
Outputs:
- interferogram: float32 [128, 2, 64, 1024], P(('groups', 'date'), None, None, 'pix'), parts along dimension 0
- coherence: float32 [128, 64, 1024], P(('groups', 'date'), None, 'pix'), parts along dimension 0
The draws below stay inside these ranges and needn't reach their ends.
There are 2 independent parts, one for each index of `groups`. The reference program is written for one: setup_inputs(seed, part) draws one part's arguments, and reference() takes and returns one part's arrays. A program takes and returns all parts, laid end to end along the dimension named above; each array names one. Nothing has to cross between parts.
Inputs may be any that keep to these rules, and one draw needn't show every extreme that they name: `pair_list`: in aligned block r of 8 rows the first column is a date of r * 2 to r * 2 + 1 and the second another date at most 6 away from it; the first row of every block is exactly 6 away. `look_sizes`: column 0 is 1 to 4, column 1 is 1 to 16; the first row of every aligned block of 8 rows holds 4 and 16.
All inputs are finite; a program needn't handle non-finite values.
Results may differ from the reference program's by a relative error of at most 0.004.
Values may be sent and summed in bfloat16 or wider, within the bound.
A program may use at most 64 MiB of HBM per device.

```python
import jax
import jax.numpy as jnp
from jax import lax

DATE_DEV = 2
AZ = 64
RBLK = 512
SPAN = 6
HA = 4
HR = 16
RANGE = 1024
DATES = 16
PAIR_DEV = 8
PAIRS = 64


def draw_slc_tiles(key, part):
    key = jax.random.fold_in(key, 11)
    weight = jax.random.uniform(jax.random.fold_in(key, 3), (DATES, 1, 1, 1), jnp.float32, 0.35, 0.9)
    amplitude = jnp.exp(jax.random.uniform(jax.random.fold_in(key, 4), (1, 1, AZ, RANGE), jnp.float32, -0.7, 0.7))
    scene = jax.random.normal(jax.random.fold_in(key, 1), (1, 2, AZ, RANGE), jnp.float32)
    noise = jax.random.normal(jax.random.fold_in(key, 2), (DATES, 2, AZ, RANGE), jnp.float32)
    mixed = amplitude * (weight * scene + jnp.sqrt(1.0 - weight * weight) * noise)
    return jnp.clip(mixed, -8.0, 8.0).astype(jnp.bfloat16)


def draw_pair_list(key, part):
    key = jax.random.fold_in(key, 12)
    row_index = jnp.arange(PAIRS, dtype=jnp.int32)
    owner = row_index // PAIR_DEV
    offset = jax.random.randint(jax.random.fold_in(key, 1), (PAIRS,), 0, DATE_DEV, dtype=jnp.int32)
    first = owner * DATE_DEV + offset
    distance = jax.random.randint(jax.random.fold_in(key, 2), (PAIRS,), 1, SPAN + 1, dtype=jnp.int32)
    distance = jnp.where(row_index % PAIR_DEV == 0, SPAN, distance)
    direction = jax.random.randint(jax.random.fold_in(key, 3), (PAIRS,), 0, 2, dtype=jnp.int32) * 2 - 1
    candidate = first + direction * distance
    second = jnp.where((candidate < 0) | (candidate >= DATES), first - direction * distance, candidate)
    return jnp.stack([first, second], 1).astype(jnp.int32)


def draw_look_sizes(key, part):
    key = jax.random.fold_in(key, 13)
    row_index = jnp.arange(PAIRS, dtype=jnp.int32)
    azimuth_half = jax.random.randint(jax.random.fold_in(key, 1), (PAIRS,), 1, HA + 1, dtype=jnp.int32)
    range_half = jax.random.randint(jax.random.fold_in(key, 2), (PAIRS,), 1, HR + 1, dtype=jnp.int32)
    leading = row_index % PAIR_DEV == 0
    azimuth_half = jnp.where(leading, HA, azimuth_half)
    range_half = jnp.where(leading, HR, range_half)
    return jnp.stack([azimuth_half, range_half], 1).astype(jnp.int32)


def with_ends(result, stream_key, smallest, largest):
    extent = result.shape
    spot = [jax.random.randint(jax.random.fold_in(stream_key, axis), (), 0, extent[axis]) for axis in range(len(extent))]
    result = result.at[tuple(spot)].set(smallest)
    longest = extent.index(max(extent))
    spot[longest] = (spot[longest] + 1) % extent[longest]
    return result.at[tuple(spot)].set(largest)


def setup_inputs(seed: int = 0, part: int = 0) -> dict:
    arg_keys = jax.random.split(jax.random.key(seed), 5)
    own_keys = jax.random.split(jax.random.fold_in(arg_keys[4], part), 5)
    slc_tiles = draw_slc_tiles(jax.random.fold_in(jax.random.fold_in(arg_keys[4], part), 71), part)
    pair_list = draw_pair_list(jax.random.fold_in(jax.random.fold_in(arg_keys[4], part), 71), part)
    band_cuts = with_ends(jax.random.randint(own_keys[2], (PAIRS, 2), 0, RBLK // 4), jax.random.fold_in(own_keys[2], 1), 0, (RBLK // 4) - 1).astype(jnp.int32)
    look_sizes = draw_look_sizes(jax.random.fold_in(jax.random.fold_in(arg_keys[4], part), 71), part)
    return {"slc_tiles": slc_tiles, "pair_list": pair_list, "band_cuts": band_cuts, "look_sizes": look_sizes}


def reference(slc_tiles, pair_list, band_cuts, look_sizes):
    values = slc_tiles.astype(jnp.float32)
    complex_tiles = values[:, 0] + 1j * values[:, 1]
    blocks = complex_tiles.reshape(DATES, AZ, RANGE // RBLK, RBLK)
    spectra = jnp.fft.fft(blocks, axis=-1)
    freq_index = (jnp.arange(RBLK, dtype=jnp.int32) + RBLK // 2) % RBLK
    columns = jnp.arange(RANGE, dtype=jnp.int32)
    azimuths = jnp.arange(AZ, dtype=jnp.int32)
    col_gap = jnp.abs(columns[:, None] - columns[None, :])
    row_gap = jnp.abs(azimuths[:, None] - azimuths[None, :])

    def filtered(which, keep_mask):
        field = jnp.fft.ifft(spectra[which] * keep_mask, axis=-1).reshape(AZ, RANGE)
        halves = jnp.stack([jnp.real(field), jnp.imag(field)]).astype(jnp.float32)
        rounded = lax.optimization_barrier(halves.astype(jnp.bfloat16))
        return rounded.astype(jnp.float32)

    def one_pair(items):
        dates_pair, cuts, halves = items
        keep_mask = ((freq_index >= cuts[0]) & (freq_index < RBLK - cuts[1])).astype(jnp.float32)
        first = filtered(dates_pair[0], keep_mask)
        second = filtered(dates_pair[1], keep_mask)
        quantity = jnp.stack([first[0] * second[0] + first[1] * second[1], first[1] * second[0] - first[0] * second[1], first[0] * first[0] + first[1] * first[1], second[0] * second[0] + second[1] * second[1]])
        range_band = (col_gap <= halves[1]).astype(jnp.float32)
        azimuth_band = (row_gap <= halves[0]).astype(jnp.float32)
        partial_sum = jnp.einsum('qac,cd->qad', quantity, range_band, precision=lax.Precision.HIGHEST)
        sums = jnp.einsum('ba,qad->qbd', azimuth_band, partial_sum, precision=lax.Precision.HIGHEST)
        window_count = ((2 * halves[0] + 1) * (2 * halves[1] + 1)).astype(jnp.float32)
        interferogram = sums[0:2] / window_count
        magnitude = jnp.sqrt(sums[0] * sums[0] + sums[1] * sums[1])
        coherence = magnitude / (jnp.sqrt(sums[2] * sums[3]) + 0.25 * window_count)
        return (interferogram, coherence)
    interferogram, coherence = lax.map(one_pair, (pair_list, band_cuts, look_sizes))
    return (interferogram, coherence)
```

```python
import functools

import jax
import jax.numpy as jnp
import numpy as np
from jax import lax
from jax.experimental import pallas as pl
from jax.experimental.pallas import tpu as pltpu
from jax.sharding import PartitionSpec as P

MESH = pl.DeviceIdType.MESH
RBLK = 512
SUB = 128
RADIX = RBLK // SUB
REACH = 3
SLOT_REL = (1, -2, 2, 3, -1, -3)


def split(x):
    high = x.astype(jnp.bfloat16)
    return high, (x - high.astype(jnp.float32)).astype(jnp.bfloat16)


def dft_tables():
    count = np.arange(SUB)
    turn = np.exp(-2j * np.pi * (np.outer(count, count) % SUB) / SUB)

    def real_form(m):
        return np.block([[m.real, m.imag], [-m.imag, m.real]]).astype(np.float32)

    def halves(m):
        high = m.astype(jnp.bfloat16)
        return np.stack([high, (m - high.astype(np.float32)).astype(jnp.bfloat16)])

    twiddle = np.exp(-2j * np.pi * np.outer(np.arange(RADIX), count) / RBLK)
    return (
        halves(real_form(turn)),
        halves(real_form(turn.conj() / RBLK)),
        np.stack([twiddle.real, twiddle.imag]).astype(np.float32),
    )


def dot(a, b):
    return jnp.dot(a, b, preferred_element_type=jnp.float32)


def dot3(high, low, table):
    return dot(high, table[0]) + dot(low, table[0]) + dot(high, table[1])


def forward(image, table, twiddle, high_ref, low_ref, index):
    rows = image.shape[1]
    re = [image[0, :, n * SUB : (n + 1) * SUB].astype(jnp.float32) for n in range(RADIX)]
    im = [image[1, :, n * SUB : (n + 1) * SUB].astype(jnp.float32) for n in range(RADIX)]
    sr, si = (re[0] + re[2], im[0] + im[2])
    dr, di = (re[0] - re[2], im[0] - im[2])
    tr, ti = (re[1] + re[3], im[1] + im[3])
    er, ei = (re[1] - re[3], im[1] - im[3])
    parts = [(sr + tr, si + ti), (dr + ei, di - er), (sr - tr, si - ti), (dr - ei, di + er)]
    turned = []
    for k, (pr, pi) in enumerate(parts):
        c, s = (twiddle[0, k : k + 1, :], twiddle[1, k : k + 1, :])
        turned.append(
            jnp.concatenate([pr, pi] if k == 0 else [pr * c - pi * s, pr * s + pi * c], 1)
        )
    high, low = split(jnp.concatenate(turned, 0))
    high, low = split(dot3(high, low, table))
    high_ref[index] = high
    low_ref[index] = low


def inverse(high, low, mask, table, twiddle, rows):
    y = dot3(high * mask, low * mask, table)
    terms = []
    for k in range(RADIX):
        pr = y[k * rows : (k + 1) * rows, :SUB]
        pi = y[k * rows : (k + 1) * rows, SUB:]
        if k:
            c, s = (twiddle[0, k : k + 1, :], twiddle[1, k : k + 1, :])
            pr, pi = (pr * c + pi * s, pi * c - pr * s)
        terms.append((pr, pi))
    (ar, ai), (br, bi), (cr, ci), (er, ei) = terms
    sr, si, dr, di = (ar + cr, ai + ci, ar - cr, ai - ci)
    tr, ti, fr, fi = (br + er, bi + ei, br - er, bi - ei)
    return [(sr + tr, si + ti), (dr - fi, di + fr), (sr - tr, si - ti), (dr + fi, di - fr)]


def field_kernel(
    dates_dev,
    pairs_ref,
    cuts_ref,
    slc_ref,
    fwd_ref,
    inv_ref,
    twiddle_ref,
    fields_ref,
    halo_ref,
    window,
    spec_high,
    spec_low,
    send_sem,
    recv_sem,
    edge_send,
    edge_recv,
):
    owned, _, rows, width = slc_ref.shape
    pair_count = pairs_ref.shape[0]
    group = lax.axis_index("groups")
    me = lax.axis_index("date")
    pix = lax.axis_index("pix")
    sign = 1 - 2 * lax.rem(me, 2)
    partner = me + sign
    ahead = me + 2 * sign
    behind = me - 2 * sign
    has_ahead = (ahead >= 0) & (ahead < dates_dev)
    has_behind = (behind >= 0) & (behind < dates_dev)
    far = me - sign
    has_far = (far >= 0) & (far < dates_dev)
    last = me - 3 * sign
    has_last = (last >= 0) & (last < dates_dev)

    barrier = pltpu.get_barrier_semaphore()

    def greet(date, pixel):
        pl.semaphore_signal(
            barrier, inc=1, device_id=(group, date, pixel), device_id_type=MESH
        )

    greet(partner, pix)
    greet(me, 1 - pix)
    pl.when(has_ahead)(lambda: greet(ahead, pix))
    pl.when(has_behind)(lambda: greet(behind, pix))
    pl.semaphore_wait(barrier, 2 + has_ahead.astype(jnp.int32) + has_behind.astype(jnp.int32))

    def copy(slot, source, d, target):
        src = slc_ref.at[d] if source is None else window.at[source, d]
        return pltpu.make_async_remote_copy(
            src_ref=src,
            dst_ref=window.at[slot, d],
            send_sem=send_sem.at[slot, d],
            recv_sem=recv_sem.at[slot, d],
            device_id=(group, target, pix),
            device_id_type=MESH,
        )

    plan = (
        (None, partner, None, None),
        (None, ahead, has_ahead, has_behind),
        (None, behind, has_behind, has_ahead),
        (0, behind, has_behind, has_ahead),
        (2, partner, has_ahead, has_far),
        (4, ahead, has_ahead & has_far, has_last),
    )

    def guarded(condition, action):
        if condition is None:
            action()
        else:
            pl.when(condition)(action)

    def send(slot, d):
        source, target, sends, _ = plan[slot]
        guarded(sends, lambda: copy(slot, source, d, target).start())

    def arrive(slot, d):
        source, target, _, receives = plan[slot]
        guarded(receives, lambda: copy(slot, source, d, target).wait_recv())

    def sent(slot, d):
        source, target, sends, _ = plan[slot]
        guarded(sends, lambda: copy(slot, source, d, target).wait_send())

    for d in range(owned):
        for slot in range(3):
            send(slot, d)

    def transform(slot, d):
        receives = plan[slot][3]

        def run():
            index = (SLOT_REL[slot] + REACH) * owned + d
            forward(window[slot, d], fwd_ref, twiddle_ref, spec_high, spec_low, index)

        guarded(receives, run)

    for d in range(owned):
        forward(slc_ref[d], fwd_ref, twiddle_ref, spec_high, spec_low, REACH * owned + d)

    line = lax.broadcasted_iota(jnp.int32, (RADIX * rows, 2 * SUB), 0)
    lane = lax.broadcasted_iota(jnp.int32, (RADIX * rows, 2 * SUB), 1)
    bins = (line // rows + RADIX * (lane % SUB) + RBLK // 2) % RBLK

    def filter_side(side):
        def step(p, carry):
            low_cut = cuts_ref[p, 0]
            high_cut = cuts_ref[p, 1]
            mask = jnp.where(
                (bins >= low_cut) & (bins < RBLK - high_cut), jnp.float32(1), jnp.float32(0)
            ).astype(jnp.bfloat16)
            date = pairs_ref[p, side]
            owner = date // owned
            index = (sign * (owner - me) + REACH) * owned + date - owner * owned
            index = jnp.clip(index, 0, spec_high.shape[0] - 1)
            tiles = inverse(spec_high[index], spec_low[index], mask, inv_ref, twiddle_ref, rows)
            for n, (re, im) in enumerate(tiles):
                fields_ref[side, p, 0, :, n * SUB : (n + 1) * SUB] = re.astype(jnp.bfloat16)
                fields_ref[side, p, 1, :, n * SUB : (n + 1) * SUB] = im.astype(jnp.bfloat16)
            return carry

        return step

    edge = pl.ds(pl.multiple_of((1 - pix) * (width - SUB), SUB), SUB)

    def edges(number, side, first, count):
        return pltpu.make_async_remote_copy(
            src_ref=fields_ref.at[side, pl.ds(first, count), :, :, edge],
            dst_ref=halo_ref.at[side, pl.ds(first, count)],
            send_sem=edge_send.at[number],
            recv_sem=edge_recv.at[number],
            device_id=(group, me, 1 - pix),
            device_id_type=MESH,
        )

    lax.fori_loop(0, pair_count, filter_side(0), 0)
    half = pair_count // 2
    edge_copies = [edges(0, 0, 0, pair_count), edges(1, 1, 0, half), edges(2, 1, half, half)]
    edge_copies[0].start()

    for d in range(owned):
        arrive(2, d)
        send(4, d)
        arrive(0, d)
        send(3, d)
    for slot in (2, 0):
        for d in range(owned):
            transform(slot, d)
    for d in range(owned):
        arrive(4, d)
        send(5, d)
    for d in range(owned):
        arrive(1, d)
        transform(1, d)
    for d in range(owned):
        transform(4, d)
    for slot in (3, 5):
        for d in range(owned):
            arrive(slot, d)
            transform(slot, d)

    lax.fori_loop(0, half, filter_side(1), 0)
    edge_copies[1].start()
    lax.fori_loop(half, pair_count, filter_side(1), 0)
    edge_copies[2].start()
    for slot in range(len(plan)):
        for d in range(owned):
            sent(slot, d)
    for item in edge_copies:
        item.wait()


def look_kernel(look_ref, fields_ref, halo_ref, interferogram_ref, coherence_ref):
    p = pl.program_id(0)
    rows, width = fields_ref.shape[-2:]
    pix = lax.axis_index("pix")
    half_az = look_ref[p, 0]
    half_range = look_ref[p, 1]

    def products(ref):
        ar, ai = (ref[0, 0, 0].astype(jnp.float32), ref[0, 0, 1].astype(jnp.float32))
        br, bi = (ref[1, 0, 0].astype(jnp.float32), ref[1, 0, 1].astype(jnp.float32))
        return split(
            jnp.concatenate(
                [ar * br + ai * bi, ai * br - ar * bi, ar * ar + ai * ai, br * br + bi * bi], 0
            )
        )

    on_left = jnp.where(pix == 1, jnp.float32(1), jnp.float32(0)).astype(jnp.bfloat16)
    on_right = jnp.where(pix == 0, jnp.float32(1), jnp.float32(0)).astype(jnp.bfloat16)
    extended = [
        jnp.concatenate([outer * on_left, inner, outer * on_right], 1)
        for inner, outer in zip(products(fields_ref), products(halo_ref))
    ]
    span = 2 * SUB
    first = lax.broadcasted_iota(jnp.int32, (span + 2 * SUB, span), 0)
    second = lax.broadcasted_iota(jnp.int32, (span + 2 * SUB, span), 1)
    one, zero = (jnp.float32(1), jnp.float32(0))
    range_band = jnp.where(jnp.abs(first - SUB - second) <= half_range, one, zero).astype(
        jnp.bfloat16
    )
    line = lax.broadcasted_iota(jnp.int32, (4 * rows, 4 * rows), 0)
    other = lax.broadcasted_iota(jnp.int32, (4 * rows, 4 * rows), 1)
    azimuth_band = jnp.where(
        (jnp.abs(line - other) <= half_az) & (line // rows == other // rows), one, zero
    ).astype(jnp.bfloat16)
    window_count = ((2 * half_az + 1) * (2 * half_range + 1)).astype(jnp.float32)
    scale = 1.0 / jnp.full((1, span), window_count, jnp.float32)
    for start in range(0, width, span):
        partial_sum = dot(extended[0][:, start : start + 2 * span], range_band) + dot(
            extended[1][:, start : start + 2 * span], range_band
        )
        high, low = split(partial_sum)
        sums = dot(azimuth_band, high) + dot(azimuth_band, low)
        re, im, first_power, second_power = [sums[q * rows : (q + 1) * rows] for q in range(4)]
        columns = slice(start, start + span)
        interferogram_ref[0, 0, :, columns] = re * scale
        interferogram_ref[0, 1, :, columns] = im * scale
        coherence_ref[0, :, columns] = jnp.sqrt(re * re + im * im) / (
            jnp.sqrt(first_power * second_power) + 0.25 * window_count
        )


def body(dates_dev, slc_tiles, pair_list, band_cuts, look_sizes):
    owned, _, rows, width = slc_tiles.shape
    pair_count = pair_list.shape[0]
    tables = [jnp.asarray(t) for t in dft_tables()]
    smem = pl.BlockSpec(memory_space=pltpu.SMEM)
    vmem = pl.BlockSpec(memory_space=pltpu.VMEM)
    slots = len(SLOT_REL)
    spectrum = (owned * (2 * REACH + 1), RADIX * rows, 2 * SUB)
    fields, halo = pl.pallas_call(
        functools.partial(field_kernel, dates_dev),
        out_shape=(
            jax.ShapeDtypeStruct((2, pair_count, 2, rows, width), jnp.bfloat16),
            jax.ShapeDtypeStruct((2, pair_count, 2, rows, SUB), jnp.bfloat16),
        ),
        in_specs=[smem, smem, vmem, vmem, vmem, vmem],
        out_specs=(vmem, vmem),
        scratch_shapes=[
            pltpu.VMEM((slots, owned, 2, rows, width), jnp.bfloat16),
            pltpu.VMEM(spectrum, jnp.bfloat16),
            pltpu.VMEM(spectrum, jnp.bfloat16),
            pltpu.SemaphoreType.DMA((slots, owned)),
            pltpu.SemaphoreType.DMA((slots, owned)),
            pltpu.SemaphoreType.DMA((3,)),
            pltpu.SemaphoreType.DMA((3,)),
        ],
        compiler_params=pltpu.CompilerParams(
            collective_id=0, has_side_effects=True, vmem_limit_bytes=40 * 1024 * 1024
        ),
        name="fields",
    )(pair_list, band_cuts, slc_tiles, *tables)
    return pl.pallas_call(
        look_kernel,
        grid=(pair_count,),
        out_shape=(
            jax.ShapeDtypeStruct((pair_count, 2, rows, width), jnp.float32),
            jax.ShapeDtypeStruct((pair_count, rows, width), jnp.float32),
        ),
        in_specs=[
            smem,
            pl.BlockSpec((2, 1, 2, rows, width), lambda p: (0, p, 0, 0, 0)),
            pl.BlockSpec((2, 1, 2, rows, SUB), lambda p: (0, p, 0, 0, 0)),
        ],
        out_specs=(
            pl.BlockSpec((1, 2, rows, width), lambda p: (p, 0, 0, 0)),
            pl.BlockSpec((1, rows, width), lambda p: (p, 0, 0)),
        ),
        compiler_params=pltpu.CompilerParams(vmem_limit_bytes=40 * 1024 * 1024),
        name="looks",
    )(look_sizes, fields, halo)


def solution(mesh):
    placed = (
        P(("groups", "date"), None, None, "pix"),
        P(("groups", "date"), None),
        P(("groups", "date"), None),
        P(("groups", "date"), None),
    )
    return jax.shard_map(
        functools.partial(body, mesh.shape["date"]),
        mesh=mesh,
        in_specs=placed,
        out_specs=(P(("groups", "date"), None, None, "pix"), P(("groups", "date"), None, "pix")),
        check_vma=False,
    )
```

```python
import functools

import jax
import jax.numpy as jnp
import numpy as np
from jax import lax
from jax.experimental import pallas as pl
from jax.experimental.pallas import tpu as pltpu
from jax.sharding import PartitionSpec as P

MESH = pl.DeviceIdType.MESH
RBLK = 512
SUB = 128
RADIX = RBLK // SUB
REACH = 3
UNROLL = 4
GROUP = 2
SLOT_REL = (1, -2, 2, 3, -1, -3)


def split(x):
    high = x.astype(jnp.bfloat16)
    return high, (x - high.astype(jnp.float32)).astype(jnp.bfloat16)


def dft_tables():
    count = np.arange(SUB)
    turn = np.exp(-2j * np.pi * (np.outer(count, count) % SUB) / SUB)

    def real_form(m):
        return np.block([[m.real, m.imag], [-m.imag, m.real]]).astype(np.float32)

    def halves(m):
        high = m.astype(jnp.bfloat16)
        return np.stack([high, (m - high.astype(np.float32)).astype(jnp.bfloat16)])

    twiddle = np.exp(-2j * np.pi * np.outer(np.arange(RADIX), count) / RBLK)
    return (
        halves(real_form(turn)),
        halves(real_form(turn.conj() / RBLK)),
        np.stack([twiddle.real, twiddle.imag]).astype(np.float32),
    )


def dot(a, b):
    return jnp.dot(a, b, preferred_element_type=jnp.float32)


def dot3(high, low, table):
    return dot(high, table[0]) + dot(low, table[0]) + dot(high, table[1])


def forward(images, table, twiddle, high_ref, low_ref, start):
    turned = []
    for image in images:
        re = [image[0, :, n * SUB : (n + 1) * SUB].astype(jnp.float32) for n in range(RADIX)]
        im = [image[1, :, n * SUB : (n + 1) * SUB].astype(jnp.float32) for n in range(RADIX)]
        sr, si = (re[0] + re[2], im[0] + im[2])
        dr, di = (re[0] - re[2], im[0] - im[2])
        tr, ti = (re[1] + re[3], im[1] + im[3])
        er, ei = (re[1] - re[3], im[1] - im[3])
        parts = [(sr + tr, si + ti), (dr + ei, di - er), (sr - tr, si - ti), (dr - ei, di + er)]
        for k, (pr, pi) in enumerate(parts):
            c, s = (twiddle[0, k : k + 1, :], twiddle[1, k : k + 1, :])
            turned.append(
                jnp.concatenate([pr, pi] if k == 0 else [pr * c - pi * s, pr * s + pi * c], 1)
            )
    high, low = split(jnp.concatenate(turned, 0))
    high, low = split(dot3(high, low, table))
    count = high.shape[0] // len(images)
    for d in range(len(images)):
        high_ref[start + d] = high[d * count : (d + 1) * count]
        low_ref[start + d] = low[d * count : (d + 1) * count]


def inverse(high, low, mask, table, twiddle, rows):
    y = dot3(high * mask, low * mask, table)
    terms = []
    for k in range(RADIX):
        pr = y[k * rows : (k + 1) * rows, :SUB]
        pi = y[k * rows : (k + 1) * rows, SUB:]
        if k:
            c, s = (twiddle[0, k : k + 1, :], twiddle[1, k : k + 1, :])
            pr, pi = (pr * c + pi * s, pi * c - pr * s)
        terms.append((pr, pi))
    (ar, ai), (br, bi), (cr, ci), (er, ei) = terms
    sr, si, dr, di = (ar + cr, ai + ci, ar - cr, ai - ci)
    tr, ti, fr, fi = (br + er, bi + ei, br - er, bi - ei)
    return [(sr + tr, si + ti), (dr - fi, di + fr), (sr - tr, si - ti), (dr + fi, di - fr)]


def field_kernel(
    dates_dev,
    pairs_ref,
    cuts_ref,
    slc_ref,
    tables_hbm,
    twiddle_hbm,
    fields_ref,
    halo_ref,
    own_ref,
    tables_ref,
    twiddle_ref,
    window,
    spec_high,
    spec_low,
    send_sem,
    recv_sem,
    edge_send,
    edge_recv,
    load_sem,
):
    owned, _, rows, width = slc_ref.shape
    pair_count = pairs_ref.shape[1]
    loads = [
        pltpu.make_async_copy(src, dst, load_sem.at[n])
        for n, (src, dst) in enumerate(
            ((slc_ref, own_ref), (tables_hbm, tables_ref), (twiddle_hbm, twiddle_ref))
        )
    ]
    for item in loads:
        item.start()
    fwd_ref, inv_ref = (tables_ref.at[0], tables_ref.at[1])
    group = lax.axis_index("groups")
    me = lax.axis_index("date")
    pix = lax.axis_index("pix")
    sign = 1 - 2 * lax.rem(me, 2)
    partner = me + sign
    ahead = me + 2 * sign
    behind = me - 2 * sign
    has_ahead = (ahead >= 0) & (ahead < dates_dev)
    has_behind = (behind >= 0) & (behind < dates_dev)
    far = me - sign
    has_far = (far >= 0) & (far < dates_dev)
    last = me - 3 * sign
    has_last = (last >= 0) & (last < dates_dev)

    barrier = pltpu.get_barrier_semaphore()

    def greet(date, pixel):
        pl.semaphore_signal(
            barrier, inc=1, device_id=(group, date, pixel), device_id_type=MESH
        )

    greet(partner, pix)
    greet(me, 1 - pix)
    pl.when(has_ahead)(lambda: greet(ahead, pix))
    pl.when(has_behind)(lambda: greet(behind, pix))
    pl.semaphore_wait(barrier, 2 + has_ahead.astype(jnp.int32) + has_behind.astype(jnp.int32))

    def copy(slot, source, d, target):
        src = slc_ref.at[d] if source is None else window.at[source, d]
        return pltpu.make_async_remote_copy(
            src_ref=src,
            dst_ref=window.at[slot, d],
            send_sem=send_sem.at[slot, d],
            recv_sem=recv_sem.at[slot, d],
            device_id=(group, target, pix),
            device_id_type=MESH,
        )

    plan = (
        (None, partner, None, None),
        (None, ahead, has_ahead, has_behind),
        (None, behind, has_behind, has_ahead),
        (0, behind, has_behind, has_ahead),
        (2, partner, has_ahead, has_far),
        (4, ahead, has_ahead & has_far, has_last),
    )

    def guarded(condition, action):
        if condition is None:
            action()
        else:
            pl.when(condition)(action)

    def send(slot, d):
        source, target, sends, _ = plan[slot]
        guarded(sends, lambda: copy(slot, source, d, target).start())

    def arrive(slot, d):
        source, target, _, receives = plan[slot]
        guarded(receives, lambda: copy(slot, source, d, target).wait_recv())

    def sent(slot, d):
        source, target, sends, _ = plan[slot]
        guarded(sends, lambda: copy(slot, source, d, target).wait_send())

    for d in range(owned):
        for slot in range(3):
            send(slot, d)

    def transform(slot):
        def run():
            images = [window[slot, d] for d in range(owned)]
            start = (SLOT_REL[slot] + REACH) * owned
            forward(images, fwd_ref, twiddle_ref, spec_high, spec_low, start)

        guarded(plan[slot][3], run)

    for item in loads:
        item.wait()
    own = [own_ref[d] for d in range(owned)]
    forward(own, fwd_ref, twiddle_ref, spec_high, spec_low, REACH * owned)

    line = lax.broadcasted_iota(jnp.int32, (RADIX * rows, 2 * SUB), 0)
    lane = lax.broadcasted_iota(jnp.int32, (RADIX * rows, 2 * SUB), 1)
    bins = (line // rows + RADIX * (lane % SUB) + RBLK // 2) % RBLK

    def filter_side(side):
        def step(p, carry):
            low_cut = cuts_ref[0, p]
            high_cut = cuts_ref[1, p]
            mask = jnp.where(
                (bins >= low_cut) & (bins < RBLK - high_cut), jnp.float32(1), jnp.float32(0)
            ).astype(jnp.bfloat16)
            date = pairs_ref[side, p]
            owner = date // owned
            index = (sign * (owner - me) + REACH) * owned + date - owner * owned
            index = jnp.clip(index, 0, spec_high.shape[0] - 1)
            tiles = inverse(spec_high[index], spec_low[index], mask, inv_ref, twiddle_ref, rows)
            for n, (re, im) in enumerate(tiles):
                fields_ref[side, p, 0, :, n * SUB : (n + 1) * SUB] = re.astype(jnp.bfloat16)
                fields_ref[side, p, 1, :, n * SUB : (n + 1) * SUB] = im.astype(jnp.bfloat16)
            return carry

        return step

    edge = pl.ds(pl.multiple_of((1 - pix) * (width - SUB), SUB), SUB)

    def edges(number, side, first, count):
        return pltpu.make_async_remote_copy(
            src_ref=fields_ref.at[side, pl.ds(first, count), :, :, edge],
            dst_ref=halo_ref.at[side, pl.ds(first, count)],
            send_sem=edge_send.at[number],
            recv_sem=edge_recv.at[number],
            device_id=(group, me, 1 - pix),
            device_id_type=MESH,
        )

    lax.fori_loop(0, pair_count, filter_side(0), 0, unroll=UNROLL)
    half = pair_count // 2
    edge_copies = [edges(0, 0, 0, pair_count), edges(1, 1, 0, half), edges(2, 1, half, half)]
    edge_copies[0].start()

    for d in range(owned):
        arrive(2, d)
        send(4, d)
        arrive(0, d)
        send(3, d)
    transform(2)
    transform(0)
    for d in range(owned):
        arrive(4, d)
        send(5, d)
    for d in range(owned):
        arrive(1, d)
    transform(1)
    transform(4)
    for slot in (3, 5):
        for d in range(owned):
            arrive(slot, d)
        transform(slot)

    lax.fori_loop(0, half, filter_side(1), 0, unroll=UNROLL)
    edge_copies[1].start()
    lax.fori_loop(half, pair_count, filter_side(1), 0, unroll=UNROLL)
    edge_copies[2].start()
    for slot in range(len(plan)):
        for d in range(owned):
            sent(slot, d)
    for item in edge_copies:
        item.wait()


def look_kernel(look_ref, fields_ref, halo_ref, interferogram_ref, coherence_ref):
    step = pl.program_id(0)
    rows, width = fields_ref.shape[-2:]
    pix = lax.axis_index("pix")

    def products(ref, g):
        ar, ai = (ref[0, g, 0].astype(jnp.float32), ref[0, g, 1].astype(jnp.float32))
        br, bi = (ref[1, g, 0].astype(jnp.float32), ref[1, g, 1].astype(jnp.float32))
        return jnp.concatenate(
            [ar * br + ai * bi, ai * br - ar * bi, ar * ar + ai * ai, br * br + bi * bi], 0
        ).astype(jnp.bfloat16)

    def root(x):
        return x * lax.rsqrt(jnp.maximum(x, jnp.float32(1e-37)))

    one, zero = (jnp.float32(1), jnp.float32(0))
    on_left = jnp.where(pix == 1, one, zero).astype(jnp.bfloat16)
    on_right = jnp.where(pix == 0, one, zero).astype(jnp.bfloat16)
    span = 2 * SUB
    first = lax.broadcasted_iota(jnp.int32, (span + 2 * SUB, span), 0)
    second = lax.broadcasted_iota(jnp.int32, (span + 2 * SUB, span), 1)
    range_gap = jnp.abs(first - SUB - second)
    line = lax.broadcasted_iota(jnp.int32, (4 * rows, 4 * rows), 0)
    other = lax.broadcasted_iota(jnp.int32, (4 * rows, 4 * rows), 1)
    azimuth_gap = jnp.where(line // rows == other // rows, jnp.abs(line - other), rows)
    for g in range(fields_ref.shape[1]):
        half_az = look_ref[0, step * fields_ref.shape[1] + g]
        half_range = look_ref[1, step * fields_ref.shape[1] + g]
        outer = products(halo_ref, g)
        extended = jnp.concatenate(
            [outer * on_left, products(fields_ref, g), outer * on_right], 1
        )
        range_band = jnp.where(range_gap <= half_range, one, zero).astype(jnp.bfloat16)
        azimuth_band = jnp.where(azimuth_gap <= half_az, one, zero).astype(jnp.bfloat16)
        window_count = ((2 * half_az + 1) * (2 * half_range + 1)).astype(jnp.float32)
        scale = 1.0 / jnp.full((1, span), window_count, jnp.float32)
        for start in range(0, width, span):
            partial_sum = dot(extended[:, start : start + 2 * span], range_band)
            sums = dot(azimuth_band, partial_sum.astype(jnp.bfloat16))
            re, im, first_power, second_power = [sums[q * rows : (q + 1) * rows] for q in range(4)]
            columns = slice(start, start + span)
            interferogram_ref[g, 0, :, columns] = re * scale
            interferogram_ref[g, 1, :, columns] = im * scale
            coherence_ref[g, :, columns] = root(re * re + im * im) / (
                root(first_power * second_power) + 0.25 * window_count
            )


def body(dates_dev, slc_tiles, pair_list, band_cuts, look_sizes):
    owned, _, rows, width = slc_tiles.shape
    pair_count = pair_list.shape[0]
    forward_table, inverse_table, twiddle = dft_tables()
    tables = jnp.asarray(np.stack([forward_table, inverse_table]))
    hbm = pl.BlockSpec(memory_space=pltpu.HBM)
    smem = pl.BlockSpec(memory_space=pltpu.SMEM)
    vmem = pl.BlockSpec(memory_space=pltpu.VMEM)
    slots = len(SLOT_REL)
    spectrum = (owned * (2 * REACH + 1), RADIX * rows, 2 * SUB)
    fields, halo = pl.pallas_call(
        functools.partial(field_kernel, dates_dev),
        out_shape=(
            jax.ShapeDtypeStruct((2, pair_count, 2, rows, width), jnp.bfloat16),
            jax.ShapeDtypeStruct((2, pair_count, 2, rows, SUB), jnp.bfloat16),
        ),
        in_specs=[smem, smem, hbm, hbm, hbm],
        out_specs=(vmem, vmem),
        scratch_shapes=[
            pltpu.VMEM(slc_tiles.shape, slc_tiles.dtype),
            pltpu.VMEM(tables.shape, tables.dtype),
            pltpu.VMEM(twiddle.shape, twiddle.dtype),
            pltpu.VMEM((slots, owned, 2, rows, width), jnp.bfloat16),
            pltpu.VMEM(spectrum, jnp.bfloat16),
            pltpu.VMEM(spectrum, jnp.bfloat16),
            pltpu.SemaphoreType.DMA((slots, owned)),
            pltpu.SemaphoreType.DMA((slots, owned)),
            pltpu.SemaphoreType.DMA((3,)),
            pltpu.SemaphoreType.DMA((3,)),
            pltpu.SemaphoreType.DMA((3,)),
        ],
        compiler_params=pltpu.CompilerParams(
            collective_id=0, has_side_effects=True, vmem_limit_bytes=40 * 1024 * 1024
        ),
        name="fields",
    )(pair_list.T, band_cuts.T, slc_tiles, tables, jnp.asarray(twiddle))
    return pl.pallas_call(
        look_kernel,
        grid=(pair_count // GROUP,),
        out_shape=(
            jax.ShapeDtypeStruct((pair_count, 2, rows, width), jnp.float32),
            jax.ShapeDtypeStruct((pair_count, rows, width), jnp.float32),
        ),
        in_specs=[
            smem,
            pl.BlockSpec((2, GROUP, 2, rows, width), lambda p: (0, p, 0, 0, 0)),
            pl.BlockSpec((2, GROUP, 2, rows, SUB), lambda p: (0, p, 0, 0, 0)),
        ],
        out_specs=(
            pl.BlockSpec((GROUP, 2, rows, width), lambda p: (p, 0, 0, 0)),
            pl.BlockSpec((GROUP, rows, width), lambda p: (p, 0, 0)),
        ),
        compiler_params=pltpu.CompilerParams(vmem_limit_bytes=40 * 1024 * 1024),
        name="looks",
    )(look_sizes.T, fields, halo)


def solution(mesh):
    placed = (
        P(("groups", "date"), None, None, "pix"),
        P(("groups", "date"), None),
        P(("groups", "date"), None),
        P(("groups", "date"), None),
    )
    return jax.shard_map(
        functools.partial(body, mesh.shape["date"]),
        mesh=mesh,
        in_specs=placed,
        out_specs=(P(("groups", "date"), None, None, "pix"), P(("groups", "date"), None, "pix")),
        check_vma=False,
    )
```

```python
import functools

import jax
import jax.numpy as jnp
import numpy as np
from jax import lax
from jax.experimental import pallas as pl
from jax.experimental.pallas import tpu as pltpu
from jax.sharding import PartitionSpec as P

MESH = pl.DeviceIdType.MESH
RBLK = 512
SUB = 128
RADIX = RBLK // SUB
REACH = 3
UNROLL = 4
GROUP = 2
SLOT_REL = (1, -2, 2, 3, -1, -3)


def split(x):
    high = x.astype(jnp.bfloat16)
    return high, (x - high.astype(jnp.float32)).astype(jnp.bfloat16)


def dft_tables():
    count = np.arange(SUB)
    turn = np.exp(-2j * np.pi * (np.outer(count, count) % SUB) / SUB)

    def real_form(m):
        return np.block([[m.real, m.imag], [-m.imag, m.real]]).astype(np.float32)

    def halves(m):
        high = m.astype(jnp.bfloat16)
        return np.stack([high, (m - high.astype(np.float32)).astype(jnp.bfloat16)])

    twiddle = np.exp(-2j * np.pi * np.outer(np.arange(RADIX), count) / RBLK)
    return (
        halves(real_form(turn)),
        halves(real_form(turn.conj() / RBLK)),
        np.stack([twiddle.real, twiddle.imag]).astype(np.float32),
    )


def dot(a, b):
    return jnp.dot(a, b, preferred_element_type=jnp.float32)


def dot3(high, low, table):
    return dot(high, table[0]) + dot(low, table[0]) + dot(high, table[1])


def forward(images, table, twiddle, high_ref, low_ref, start):
    turned = []
    for image in images:
        re = [image[0, :, n * SUB : (n + 1) * SUB].astype(jnp.float32) for n in range(RADIX)]
        im = [image[1, :, n * SUB : (n + 1) * SUB].astype(jnp.float32) for n in range(RADIX)]
        sr, si = (re[0] + re[2], im[0] + im[2])
        dr, di = (re[0] - re[2], im[0] - im[2])
        tr, ti = (re[1] + re[3], im[1] + im[3])
        er, ei = (re[1] - re[3], im[1] - im[3])
        parts = [(sr + tr, si + ti), (dr + ei, di - er), (sr - tr, si - ti), (dr - ei, di + er)]
        for k, (pr, pi) in enumerate(parts):
            c, s = (twiddle[0, k : k + 1, :], twiddle[1, k : k + 1, :])
            turned.append(
                jnp.concatenate([pr, pi] if k == 0 else [pr * c - pi * s, pr * s + pi * c], 1)
            )
    high, low = split(jnp.concatenate(turned, 0))
    high, low = split(dot3(high, low, table))
    count = high.shape[0] // len(images)
    for d in range(len(images)):
        high_ref[start + d] = high[d * count : (d + 1) * count]
        low_ref[start + d] = low[d * count : (d + 1) * count]


def inverse(high, low, mask, table, twiddle, rows):
    y = dot3(high * mask, low * mask, table)
    terms = []
    for k in range(RADIX):
        pr = y[k * rows : (k + 1) * rows, :SUB]
        pi = y[k * rows : (k + 1) * rows, SUB:]
        if k:
            c, s = (twiddle[0, k : k + 1, :], twiddle[1, k : k + 1, :])
            pr, pi = (pr * c + pi * s, pi * c - pr * s)
        terms.append((pr, pi))
    (ar, ai), (br, bi), (cr, ci), (er, ei) = terms
    sr, si, dr, di = (ar + cr, ai + ci, ar - cr, ai - ci)
    tr, ti, fr, fi = (br + er, bi + ei, br - er, bi - ei)
    return [(sr + tr, si + ti), (dr - fi, di + fr), (sr - tr, si - ti), (dr + fi, di - fr)]


def field_kernel(
    dates_dev,
    pairs_ref,
    cuts_ref,
    slc_ref,
    tables_hbm,
    twiddle_hbm,
    fields_ref,
    halo_ref,
    own_ref,
    tables_ref,
    twiddle_ref,
    window,
    spec_high,
    spec_low,
    send_sem,
    recv_sem,
    edge_send,
    edge_recv,
    load_sem,
):
    owned, _, rows, width = slc_ref.shape
    pair_count = pairs_ref.shape[1]
    loads = [
        pltpu.make_async_copy(src, dst, load_sem.at[n])
        for n, (src, dst) in enumerate(
            ((slc_ref, own_ref), (tables_hbm, tables_ref), (twiddle_hbm, twiddle_ref))
        )
    ]
    for item in loads:
        item.start()
    fwd_ref, inv_ref = (tables_ref.at[0], tables_ref.at[1])
    group = lax.axis_index("groups")
    me = lax.axis_index("date")
    pix = lax.axis_index("pix")
    sign = 1 - 2 * lax.rem(me, 2)
    partner = me + sign
    ahead = me + 2 * sign
    behind = me - 2 * sign
    has_ahead = (ahead >= 0) & (ahead < dates_dev)
    has_behind = (behind >= 0) & (behind < dates_dev)
    far = me - sign
    has_far = (far >= 0) & (far < dates_dev)
    last = me - 3 * sign
    has_last = (last >= 0) & (last < dates_dev)

    barrier = pltpu.get_barrier_semaphore()

    def greet(date, pixel):
        pl.semaphore_signal(
            barrier, inc=1, device_id=(group, date, pixel), device_id_type=MESH
        )

    greet(partner, pix)
    greet(me, 1 - pix)
    pl.when(has_ahead)(lambda: greet(ahead, pix))
    pl.when(has_behind)(lambda: greet(behind, pix))
    pl.semaphore_wait(barrier, 2 + has_ahead.astype(jnp.int32) + has_behind.astype(jnp.int32))

    def copy(slot, source, c, target):
        d, half = divmod(c, 2)
        src = slc_ref.at[d, half] if source is None else window.at[source, d, half]
        return pltpu.make_async_remote_copy(
            src_ref=src,
            dst_ref=window.at[slot, d, half],
            send_sem=send_sem.at[slot, c],
            recv_sem=recv_sem.at[slot, c],
            device_id=(group, target, pix),
            device_id_type=MESH,
        )

    plan = (
        (None, partner, None, None),
        (None, ahead, has_ahead, has_behind),
        (None, behind, has_behind, has_ahead),
        (0, behind, has_behind, has_ahead),
        (2, partner, has_ahead, has_far),
        (4, ahead, has_ahead & has_far, has_last),
    )

    def guarded(condition, action):
        if condition is None:
            action()
        else:
            pl.when(condition)(action)

    def send(slot, d):
        source, target, sends, _ = plan[slot]
        guarded(sends, lambda: copy(slot, source, d, target).start())

    def arrive(slot, d):
        source, target, _, receives = plan[slot]
        guarded(receives, lambda: copy(slot, source, d, target).wait_recv())

    def sent(slot, d):
        source, target, sends, _ = plan[slot]
        guarded(sends, lambda: copy(slot, source, d, target).wait_send())

    chunks = 2 * owned
    for c in range(chunks):
        for slot in (2, 1, 0):
            send(slot, c)

    def transform(slot):
        def run():
            images = [window[slot, d] for d in range(owned)]
            start = (SLOT_REL[slot] + REACH) * owned
            forward(images, fwd_ref, twiddle_ref, spec_high, spec_low, start)

        guarded(plan[slot][3], run)

    for item in loads:
        item.wait()
    own = [own_ref[d] for d in range(owned)]
    forward(own, fwd_ref, twiddle_ref, spec_high, spec_low, REACH * owned)

    line = lax.broadcasted_iota(jnp.int32, (RADIX * rows, 2 * SUB), 0)
    lane = lax.broadcasted_iota(jnp.int32, (RADIX * rows, 2 * SUB), 1)
    bins = (line // rows + RADIX * (lane % SUB) + RBLK // 2) % RBLK

    def filter_side(side):
        def step(p, carry):
            low_cut = cuts_ref[0, p]
            high_cut = cuts_ref[1, p]
            mask = jnp.where(
                (bins >= low_cut) & (bins < RBLK - high_cut), jnp.float32(1), jnp.float32(0)
            ).astype(jnp.bfloat16)
            date = pairs_ref[side, p]
            owner = date // owned
            index = (sign * (owner - me) + REACH) * owned + date - owner * owned
            index = jnp.clip(index, 0, spec_high.shape[0] - 1)
            tiles = inverse(spec_high[index], spec_low[index], mask, inv_ref, twiddle_ref, rows)
            for n, (re, im) in enumerate(tiles):
                fields_ref[side, p, 0, :, n * SUB : (n + 1) * SUB] = re.astype(jnp.bfloat16)
                fields_ref[side, p, 1, :, n * SUB : (n + 1) * SUB] = im.astype(jnp.bfloat16)
            return carry

        return step

    edge = pl.ds(pl.multiple_of((1 - pix) * (width - SUB), SUB), SUB)

    def edges(number, side, first, count):
        return pltpu.make_async_remote_copy(
            src_ref=fields_ref.at[side, pl.ds(first, count), :, :, edge],
            dst_ref=halo_ref.at[side, pl.ds(first, count)],
            send_sem=edge_send.at[number],
            recv_sem=edge_recv.at[number],
            device_id=(group, me, 1 - pix),
            device_id_type=MESH,
        )

    half = pair_count // 2
    edge_copies = [edges(0, 0, 0, pair_count), edges(1, 1, 0, half), edges(2, 1, half, half)]
    def relay(c):
        arrive(4, c)
        send(5, c)

    share = pair_count // chunks
    for c in range(chunks):
        lax.fori_loop(c * share, (c + 1) * share, filter_side(0), 0, unroll=2)
        arrive(2, c)
        send(4, c)
        arrive(0, c)
        send(3, c)
        if c >= 2:
            relay(c - 2)
    edge_copies[0].start()
    relay(chunks - 2)
    transform(2)
    relay(chunks - 1)
    transform(0)
    for c in range(chunks):
        arrive(1, c)
    transform(1)
    transform(4)
    for slot in (3, 5):
        for c in range(chunks):
            arrive(slot, c)
        transform(slot)

    lax.fori_loop(0, half, filter_side(1), 0, unroll=UNROLL)
    edge_copies[1].start()
    lax.fori_loop(half, pair_count, filter_side(1), 0, unroll=UNROLL)
    edge_copies[2].start()
    for slot in range(len(plan)):
        for c in range(chunks):
            sent(slot, c)
    for item in edge_copies:
        item.wait()


def look_kernel(look_ref, fields_ref, halo_ref, interferogram_ref, coherence_ref):
    step = pl.program_id(0)
    rows, width = fields_ref.shape[-2:]
    pix = lax.axis_index("pix")

    def products(ref, g):
        ar, ai = (ref[0, g, 0].astype(jnp.float32), ref[0, g, 1].astype(jnp.float32))
        br, bi = (ref[1, g, 0].astype(jnp.float32), ref[1, g, 1].astype(jnp.float32))
        return jnp.concatenate(
            [ar * br + ai * bi, ai * br - ar * bi, ar * ar + ai * ai, br * br + bi * bi], 0
        ).astype(jnp.bfloat16)

    def root(x):
        return x * lax.rsqrt(jnp.maximum(x, jnp.float32(1e-37)))

    one, zero = (jnp.float32(1), jnp.float32(0))
    on_left = jnp.where(pix == 1, one, zero).astype(jnp.bfloat16)
    on_right = jnp.where(pix == 0, one, zero).astype(jnp.bfloat16)
    span = 2 * SUB
    first = lax.broadcasted_iota(jnp.int32, (span + 2 * SUB, span), 0)
    second = lax.broadcasted_iota(jnp.int32, (span + 2 * SUB, span), 1)
    range_gap = jnp.abs(first - SUB - second)
    line = lax.broadcasted_iota(jnp.int32, (4 * rows, 4 * rows), 0)
    other = lax.broadcasted_iota(jnp.int32, (4 * rows, 4 * rows), 1)
    azimuth_gap = jnp.where(line // rows == other // rows, jnp.abs(line - other), rows)
    for g in range(fields_ref.shape[1]):
        half_az = look_ref[0, step * fields_ref.shape[1] + g]
        half_range = look_ref[1, step * fields_ref.shape[1] + g]
        outer = products(halo_ref, g)
        extended = jnp.concatenate(
            [outer * on_left, products(fields_ref, g), outer * on_right], 1
        )
        range_band = jnp.where(range_gap <= half_range, one, zero).astype(jnp.bfloat16)
        azimuth_band = jnp.where(azimuth_gap <= half_az, one, zero).astype(jnp.bfloat16)
        window_count = ((2 * half_az + 1) * (2 * half_range + 1)).astype(jnp.float32)
        scale = 1.0 / jnp.full((1, span), window_count, jnp.float32)
        for start in range(0, width, span):
            partial_sum = dot(extended[:, start : start + 2 * span], range_band)
            sums = dot(azimuth_band, partial_sum.astype(jnp.bfloat16))
            re, im, first_power, second_power = [sums[q * rows : (q + 1) * rows] for q in range(4)]
            columns = slice(start, start + span)
            interferogram_ref[g, 0, :, columns] = re * scale
            interferogram_ref[g, 1, :, columns] = im * scale
            coherence_ref[g, :, columns] = root(re * re + im * im) / (
                root(first_power * second_power) + 0.25 * window_count
            )


def body(dates_dev, slc_tiles, pair_list, band_cuts, look_sizes):
    owned, _, rows, width = slc_tiles.shape
    pair_count = pair_list.shape[0]
    forward_table, inverse_table, twiddle = dft_tables()
    tables = jnp.asarray(np.stack([forward_table, inverse_table]))
    hbm = pl.BlockSpec(memory_space=pltpu.HBM)
    smem = pl.BlockSpec(memory_space=pltpu.SMEM)
    vmem = pl.BlockSpec(memory_space=pltpu.VMEM)
    slots = len(SLOT_REL)
    spectrum = (owned * (2 * REACH + 1), RADIX * rows, 2 * SUB)
    fields, halo = pl.pallas_call(
        functools.partial(field_kernel, dates_dev),
        out_shape=(
            jax.ShapeDtypeStruct((2, pair_count, 2, rows, width), jnp.bfloat16),
            jax.ShapeDtypeStruct((2, pair_count, 2, rows, SUB), jnp.bfloat16),
        ),
        in_specs=[smem, smem, hbm, hbm, hbm],
        out_specs=(vmem, vmem),
        scratch_shapes=[
            pltpu.VMEM(slc_tiles.shape, slc_tiles.dtype),
            pltpu.VMEM(tables.shape, tables.dtype),
            pltpu.VMEM(twiddle.shape, twiddle.dtype),
            pltpu.VMEM((slots, owned, 2, rows, width), jnp.bfloat16),
            pltpu.VMEM(spectrum, jnp.bfloat16),
            pltpu.VMEM(spectrum, jnp.bfloat16),
            pltpu.SemaphoreType.DMA((slots, 2 * owned)),
            pltpu.SemaphoreType.DMA((slots, 2 * owned)),
            pltpu.SemaphoreType.DMA((3,)),
            pltpu.SemaphoreType.DMA((3,)),
            pltpu.SemaphoreType.DMA((3,)),
        ],
        compiler_params=pltpu.CompilerParams(
            collective_id=0, has_side_effects=True, vmem_limit_bytes=56 * 1024 * 1024
        ),
        name="fields",
    )(pair_list.T, band_cuts.T, slc_tiles, tables, jnp.asarray(twiddle))
    return pl.pallas_call(
        look_kernel,
        grid=(pair_count // GROUP,),
        out_shape=(
            jax.ShapeDtypeStruct((pair_count, 2, rows, width), jnp.float32),
            jax.ShapeDtypeStruct((pair_count, rows, width), jnp.float32),
        ),
        in_specs=[
            smem,
            pl.BlockSpec((2, GROUP, 2, rows, width), lambda p: (0, p, 0, 0, 0)),
            pl.BlockSpec((2, GROUP, 2, rows, SUB), lambda p: (0, p, 0, 0, 0)),
        ],
        out_specs=(
            pl.BlockSpec((GROUP, 2, rows, width), lambda p: (p, 0, 0, 0)),
            pl.BlockSpec((GROUP, rows, width), lambda p: (p, 0, 0)),
        ),
        compiler_params=pltpu.CompilerParams(vmem_limit_bytes=56 * 1024 * 1024),
        name="looks",
    )(look_sizes.T, fields, halo)


def solution(mesh):
    placed = (
        P(("groups", "date"), None, None, "pix"),
        P(("groups", "date"), None),
        P(("groups", "date"), None),
        P(("groups", "date"), None),
    )
    return jax.shard_map(
        functools.partial(body, mesh.shape["date"]),
        mesh=mesh,
        in_specs=placed,
        out_specs=(P(("groups", "date"), None, None, "pix"), P(("groups", "date"), None, "pix")),
        check_vma=False,
    )
```

```python
import functools

import jax
import jax.numpy as jnp
import numpy as np
from jax import lax
from jax.experimental import pallas as pl
from jax.experimental.pallas import tpu as pltpu
from jax.sharding import PartitionSpec as P

MESH = pl.DeviceIdType.MESH
RBLK = 512
SUB = 128
RADIX = RBLK // SUB
REACH = 3
UNROLL = 4
GROUP = 4
SLOT_REL = (1, -2, 2, 3, -1, -3)


def split(x):
    high = x.astype(jnp.bfloat16)
    return high, (x - high.astype(jnp.float32)).astype(jnp.bfloat16)


def dft_tables():
    count = np.arange(SUB)
    turn = np.exp(-2j * np.pi * (np.outer(count, count) % SUB) / SUB)

    def real_form(m):
        return np.block([[m.real, m.imag], [-m.imag, m.real]]).astype(np.float32)

    def halves(m):
        high = m.astype(jnp.bfloat16)
        return np.stack([high, (m - high.astype(np.float32)).astype(jnp.bfloat16)])

    twiddle = np.exp(-2j * np.pi * np.outer(np.arange(RADIX), count) / RBLK)
    return (
        halves(real_form(turn)),
        halves(real_form(turn.conj() / RBLK)),
        np.stack([twiddle.real, twiddle.imag]).astype(np.float32),
    )


def dot(a, b):
    return jnp.dot(a, b, preferred_element_type=jnp.float32)


def dot3(high, low, table):
    return dot(high, table[0]) + dot(low, table[0]) + dot(high, table[1])


def forward(images, table, twiddle, high_ref, low_ref, start):
    turned = []
    for image in images:
        re = [image[0, :, n * SUB : (n + 1) * SUB].astype(jnp.float32) for n in range(RADIX)]
        im = [image[1, :, n * SUB : (n + 1) * SUB].astype(jnp.float32) for n in range(RADIX)]
        sr, si = (re[0] + re[2], im[0] + im[2])
        dr, di = (re[0] - re[2], im[0] - im[2])
        tr, ti = (re[1] + re[3], im[1] + im[3])
        er, ei = (re[1] - re[3], im[1] - im[3])
        parts = [(sr + tr, si + ti), (dr + ei, di - er), (sr - tr, si - ti), (dr - ei, di + er)]
        for k, (pr, pi) in enumerate(parts):
            c, s = (twiddle[0, k : k + 1, :], twiddle[1, k : k + 1, :])
            turned.append(
                jnp.concatenate([pr, pi] if k == 0 else [pr * c - pi * s, pr * s + pi * c], 1)
            )
    high, low = split(jnp.concatenate(turned, 0))
    high, low = split(dot3(high, low, table))
    count = high.shape[0] // len(images)
    for d in range(len(images)):
        high_ref[start + d] = high[d * count : (d + 1) * count]
        low_ref[start + d] = low[d * count : (d + 1) * count]


def inverse(high, low, mask, table, twiddle, rows):
    y = dot3(high * mask, low * mask, table)
    terms = []
    for k in range(RADIX):
        pr = y[k * rows : (k + 1) * rows, :SUB]
        pi = y[k * rows : (k + 1) * rows, SUB:]
        if k:
            c, s = (twiddle[0, k : k + 1, :], twiddle[1, k : k + 1, :])
            pr, pi = (pr * c + pi * s, pi * c - pr * s)
        terms.append((pr, pi))
    (ar, ai), (br, bi), (cr, ci), (er, ei) = terms
    sr, si, dr, di = (ar + cr, ai + ci, ar - cr, ai - ci)
    tr, ti, fr, fi = (br + er, bi + ei, br - er, bi - ei)
    return [(sr + tr, si + ti), (dr - fi, di + fr), (sr - tr, si - ti), (dr + fi, di - fr)]


def field_kernel(
    dates_dev,
    pairs_ref,
    cuts_ref,
    slc_ref,
    tables_hbm,
    twiddle_hbm,
    fields_ref,
    halo_ref,
    own_ref,
    tables_ref,
    twiddle_ref,
    window,
    spec_high,
    spec_low,
    send_sem,
    recv_sem,
    edge_send,
    edge_recv,
    load_sem,
):
    owned, _, rows, width = slc_ref.shape
    pair_count = pairs_ref.shape[1]
    loads = [
        pltpu.make_async_copy(src, dst, load_sem.at[n])
        for n, (src, dst) in enumerate(
            ((slc_ref, own_ref), (tables_hbm, tables_ref), (twiddle_hbm, twiddle_ref))
        )
    ]
    for item in loads:
        item.start()
    fwd_ref, inv_ref = (tables_ref.at[0], tables_ref.at[1])
    group = lax.axis_index("groups")
    me = lax.axis_index("date")
    pix = lax.axis_index("pix")
    sign = 1 - 2 * lax.rem(me, 2)
    partner = me + sign
    ahead = me + 2 * sign
    behind = me - 2 * sign
    has_ahead = (ahead >= 0) & (ahead < dates_dev)
    has_behind = (behind >= 0) & (behind < dates_dev)
    far = me - sign
    has_far = (far >= 0) & (far < dates_dev)
    last = me - 3 * sign
    has_last = (last >= 0) & (last < dates_dev)

    barrier = pltpu.get_barrier_semaphore()

    def greet(date, pixel):
        pl.semaphore_signal(
            barrier, inc=1, device_id=(group, date, pixel), device_id_type=MESH
        )

    greet(partner, pix)
    greet(me, 1 - pix)
    pl.when(has_ahead)(lambda: greet(ahead, pix))
    pl.when(has_behind)(lambda: greet(behind, pix))
    pl.semaphore_wait(barrier, 2 + has_ahead.astype(jnp.int32) + has_behind.astype(jnp.int32))

    def copy(slot, source, c, target):
        d, half = divmod(c, 2)
        src = slc_ref.at[d, half] if source is None else window.at[source, d, half]
        return pltpu.make_async_remote_copy(
            src_ref=src,
            dst_ref=window.at[slot, d, half],
            send_sem=send_sem.at[slot, c],
            recv_sem=recv_sem.at[slot, c],
            device_id=(group, target, pix),
            device_id_type=MESH,
        )

    plan = (
        (None, partner, None, None),
        (None, ahead, has_ahead, has_behind),
        (None, behind, has_behind, has_ahead),
        (0, behind, has_behind, has_ahead),
        (2, partner, has_ahead, has_far),
        (4, ahead, has_ahead & has_far, has_last),
    )

    def guarded(condition, action):
        if condition is None:
            action()
        else:
            pl.when(condition)(action)

    def send(slot, d):
        source, target, sends, _ = plan[slot]
        guarded(sends, lambda: copy(slot, source, d, target).start())

    def arrive(slot, d):
        source, target, _, receives = plan[slot]
        guarded(receives, lambda: copy(slot, source, d, target).wait_recv())

    def sent(slot, d):
        source, target, sends, _ = plan[slot]
        guarded(sends, lambda: copy(slot, source, d, target).wait_send())

    chunks = 2 * owned
    for c in range(chunks):
        for slot in (2, 1, 0):
            send(slot, c)

    def transform(slot):
        def run():
            images = [window[slot, d] for d in range(owned)]
            start = (SLOT_REL[slot] + REACH) * owned
            forward(images, fwd_ref, twiddle_ref, spec_high, spec_low, start)

        guarded(plan[slot][3], run)

    for item in loads:
        item.wait()
    own = [own_ref[d] for d in range(owned)]
    forward(own, fwd_ref, twiddle_ref, spec_high, spec_low, REACH * owned)

    line = lax.broadcasted_iota(jnp.int32, (RADIX * rows, 2 * SUB), 0)
    lane = lax.broadcasted_iota(jnp.int32, (RADIX * rows, 2 * SUB), 1)
    bins = (line // rows + RADIX * (lane % SUB) + RBLK // 2) % RBLK

    def filter_side(side):
        def step(p, carry):
            low_cut = cuts_ref[0, p]
            high_cut = cuts_ref[1, p]
            mask = jnp.where(
                (bins >= low_cut) & (bins < RBLK - high_cut), jnp.float32(1), jnp.float32(0)
            ).astype(jnp.bfloat16)
            date = pairs_ref[side, p]
            owner = date // owned
            index = (sign * (owner - me) + REACH) * owned + date - owner * owned
            index = jnp.clip(index, 0, spec_high.shape[0] - 1)
            tiles = inverse(spec_high[index], spec_low[index], mask, inv_ref, twiddle_ref, rows)
            for n, (re, im) in enumerate(tiles):
                fields_ref[side, p, 0, :, n * SUB : (n + 1) * SUB] = re.astype(jnp.bfloat16)
                fields_ref[side, p, 1, :, n * SUB : (n + 1) * SUB] = im.astype(jnp.bfloat16)
            return carry

        return step

    edge = pl.ds(pl.multiple_of((1 - pix) * (width - SUB), SUB), SUB)

    def edges(number, side, first, count):
        return pltpu.make_async_remote_copy(
            src_ref=fields_ref.at[side, pl.ds(first, count), :, :, edge],
            dst_ref=halo_ref.at[side, pl.ds(first, count)],
            send_sem=edge_send.at[number],
            recv_sem=edge_recv.at[number],
            device_id=(group, me, 1 - pix),
            device_id_type=MESH,
        )

    half = pair_count // 2
    edge_copies = [edges(0, 0, 0, pair_count), edges(1, 1, 0, half), edges(2, 1, half, half)]
    def relay(c):
        arrive(4, c)
        send(5, c)

    share = pair_count // chunks
    for c in range(chunks):
        lax.fori_loop(c * share, (c + 1) * share, filter_side(0), 0, unroll=2)
        arrive(2, c)
        send(4, c)
        arrive(0, c)
        send(3, c)
        if c >= 2:
            relay(c - 2)
    edge_copies[0].start()
    relay(chunks - 2)
    transform(2)
    relay(chunks - 1)
    transform(0)
    for c in range(chunks):
        arrive(1, c)
    transform(1)
    transform(4)
    for slot in (3, 5):
        for c in range(chunks):
            arrive(slot, c)
        transform(slot)

    lax.fori_loop(0, half, filter_side(1), 0, unroll=UNROLL)
    edge_copies[1].start()
    lax.fori_loop(half, pair_count, filter_side(1), 0, unroll=UNROLL)
    edge_copies[2].start()
    for slot in range(len(plan)):
        for c in range(chunks):
            sent(slot, c)
    for item in edge_copies:
        item.wait()


def look_kernel(look_ref, fields_ref, halo_ref, interferogram_ref, coherence_ref):
    step = pl.program_id(0)
    rows, width = fields_ref.shape[-2:]
    pix = lax.axis_index("pix")

    def products(ref, g):
        ar, ai = (ref[0, g, 0].astype(jnp.float32), ref[0, g, 1].astype(jnp.float32))
        br, bi = (ref[1, g, 0].astype(jnp.float32), ref[1, g, 1].astype(jnp.float32))
        return jnp.concatenate(
            [ar * br + ai * bi, ai * br - ar * bi, ar * ar + ai * ai, br * br + bi * bi], 0
        ).astype(jnp.bfloat16)

    def root(x):
        return x * lax.rsqrt(jnp.maximum(x, jnp.float32(1e-37)))

    one, zero = (jnp.float32(1), jnp.float32(0))
    on_left = jnp.where(pix == 1, one, zero).astype(jnp.bfloat16)
    on_right = jnp.where(pix == 0, one, zero).astype(jnp.bfloat16)
    span = 2 * SUB
    first = lax.broadcasted_iota(jnp.int32, (span + 2 * SUB, span), 0)
    second = lax.broadcasted_iota(jnp.int32, (span + 2 * SUB, span), 1)
    range_gap = jnp.abs(first - SUB - second)
    line = lax.broadcasted_iota(jnp.int32, (4 * rows, 4 * rows), 0)
    other = lax.broadcasted_iota(jnp.int32, (4 * rows, 4 * rows), 1)
    azimuth_gap = jnp.where(line // rows == other // rows, jnp.abs(line - other), rows)
    for g in range(fields_ref.shape[1]):
        half_az = look_ref[0, step * fields_ref.shape[1] + g]
        half_range = look_ref[1, step * fields_ref.shape[1] + g]
        outer = products(halo_ref, g)
        extended = jnp.concatenate(
            [outer * on_left, products(fields_ref, g), outer * on_right], 1
        )
        range_band = jnp.where(range_gap <= half_range, one, zero).astype(jnp.bfloat16)
        azimuth_band = jnp.where(azimuth_gap <= half_az, one, zero).astype(jnp.bfloat16)
        window_count = ((2 * half_az + 1) * (2 * half_range + 1)).astype(jnp.float32)
        scale = 1.0 / jnp.full((1, span), window_count, jnp.float32)
        for start in range(0, width, span):
            partial_sum = dot(extended[:, start : start + 2 * span], range_band)
            sums = dot(azimuth_band, partial_sum.astype(jnp.bfloat16))
            re, im, first_power, second_power = [sums[q * rows : (q + 1) * rows] for q in range(4)]
            columns = slice(start, start + span)
            interferogram_ref[g, 0, :, columns] = re * scale
            interferogram_ref[g, 1, :, columns] = im * scale
            coherence_ref[g, :, columns] = root(re * re + im * im) / (
                root(first_power * second_power) + 0.25 * window_count
            )


def body(dates_dev, slc_tiles, pair_list, band_cuts, look_sizes):
    owned, _, rows, width = slc_tiles.shape
    pair_count = pair_list.shape[0]
    forward_table, inverse_table, twiddle = dft_tables()
    tables = jnp.asarray(np.stack([forward_table, inverse_table]))
    hbm = pl.BlockSpec(memory_space=pltpu.HBM)
    smem = pl.BlockSpec(memory_space=pltpu.SMEM)
    vmem = pl.BlockSpec(memory_space=pltpu.VMEM)
    slots = len(SLOT_REL)
    spectrum = (owned * (2 * REACH + 1), RADIX * rows, 2 * SUB)
    fields, halo = pl.pallas_call(
        functools.partial(field_kernel, dates_dev),
        out_shape=(
            jax.ShapeDtypeStruct((2, pair_count, 2, rows, width), jnp.bfloat16),
            jax.ShapeDtypeStruct((2, pair_count, 2, rows, SUB), jnp.bfloat16),
        ),
        in_specs=[smem, smem, hbm, hbm, hbm],
        out_specs=(vmem, vmem),
        scratch_shapes=[
            pltpu.VMEM(slc_tiles.shape, slc_tiles.dtype),
            pltpu.VMEM(tables.shape, tables.dtype),
            pltpu.VMEM(twiddle.shape, twiddle.dtype),
            pltpu.VMEM((slots, owned, 2, rows, width), jnp.bfloat16),
            pltpu.VMEM(spectrum, jnp.bfloat16),
            pltpu.VMEM(spectrum, jnp.bfloat16),
            pltpu.SemaphoreType.DMA((slots, 2 * owned)),
            pltpu.SemaphoreType.DMA((slots, 2 * owned)),
            pltpu.SemaphoreType.DMA((3,)),
            pltpu.SemaphoreType.DMA((3,)),
            pltpu.SemaphoreType.DMA((3,)),
        ],
        compiler_params=pltpu.CompilerParams(
            collective_id=0, has_side_effects=True, vmem_limit_bytes=56 * 1024 * 1024
        ),
        name="fields",
    )(pair_list.T, band_cuts.T, slc_tiles, tables, jnp.asarray(twiddle))
    return pl.pallas_call(
        look_kernel,
        grid=(pair_count // GROUP,),
        out_shape=(
            jax.ShapeDtypeStruct((pair_count, 2, rows, width), jnp.float32),
            jax.ShapeDtypeStruct((pair_count, rows, width), jnp.float32),
        ),
        in_specs=[
            smem,
            pl.BlockSpec((2, GROUP, 2, rows, width), lambda p: (0, p, 0, 0, 0)),
            pl.BlockSpec((2, GROUP, 2, rows, SUB), lambda p: (0, p, 0, 0, 0)),
        ],
        out_specs=(
            pl.BlockSpec((GROUP, 2, rows, width), lambda p: (p, 0, 0, 0)),
            pl.BlockSpec((GROUP, rows, width), lambda p: (p, 0, 0)),
        ),
        compiler_params=pltpu.CompilerParams(vmem_limit_bytes=56 * 1024 * 1024),
        name="looks",
    )(look_sizes.T, fields, halo)


def solution(mesh):
    placed = (
        P(("groups", "date"), None, None, "pix"),
        P(("groups", "date"), None),
        P(("groups", "date"), None),
        P(("groups", "date"), None),
    )
    return jax.shard_map(
        functools.partial(body, mesh.shape["date"]),
        mesh=mesh,
        in_specs=placed,
        out_specs=(P(("groups", "date"), None, None, "pix"), P(("groups", "date"), None, "pix")),
        check_vma=False,
    )
```
